768 devices in a mesh: tok: 16 (over x, y_lo), feat: 48 (over z, y_hi, core).
Axes of the slice: x: 4, y: 8 (y_hi: 2, y_lo: 4; y = y_hi * 4 + y_lo), z: 12, core: 2. Of those that a mesh axis runs over, the one named last changes fastest.
Arguments:
- source_acts: bfloat16 [3072, 4096], P('tok'), may hold values from -6 to 6
- target_acts: bfloat16 [3072, 4096], P('tok'), may hold values from -6 to 6
- enc_weight: bfloat16 [4096, 18432], P(None, 'feat'), may hold values from -0.09375 to 0.09375
- enc_bias: float32 [18432], P('feat'), may hold values from -1 to 1
- dec_weight: bfloat16 [18432, 4096], P('feat'), may hold values from -0.125 to 0.125
- active_blocks: int32 [48, 48], P('tok'), may hold values from 0 to 143, all different within a row
Outputs:
- grad_encoder: float32 [4096, 18432], P('tok', 'feat')
- grad_decoder: float32 [18432, 4096], P('feat', 'tok')
- recon_loss: float32 [], replicated
The draws below stay inside these ranges and needn't reach their ends.
Inputs may be any that keep to these rules, and one draw needn't show every extreme that they name: `active_blocks`: each row lists 48 different blocks, and every block is listed by some row.
All inputs are finite; a program needn't handle non-finite values.
Results may differ from the reference program's by a relative error of at most 0.02.
Values may be sent and summed in bfloat16 or wider, within the bound.
A program may use at most 64 MiB of HBM per device.

```python
import jax
import jax.numpy as jnp
from jax import lax

D = 4096
F = 18432
BLOCK = 128
TILE = 64
K = 48
TOK_DEV = 192
TOKENS = 3072
N_TOK = 16


def steps_of(own_key, extent, shards, low, high):
    factor_of, own = 1.0, jax.random.fold_in(own_key, 6)
    for position, parts in shards:
        draws = jnp.exp(jax.random.uniform(jax.random.fold_in(own, position), (parts,), jnp.float32, low / len(shards), high / len(shards)))
        factor_of = factor_of * jnp.repeat(draws, extent[position] // parts).reshape([-1 if axis == position else 1 for axis in range(len(extent))])
    return factor_of


def distinct(rng, rows, count, top, lift):
    order = jax.random.permutation(jax.random.fold_in(rng, 1), count)
    pull = order
    for power in range(3):
        pull = pull * pull // count
    pull = pull * lift // count
    chance = jax.random.randint(jax.random.fold_in(rng, 2), (rows, count), 0, 4096) + pull
    fixed_rows = jax.random.permutation(jax.random.fold_in(rng, 3), rows)[jnp.arange(count) % rows]
    chance = jnp.where(jnp.arange(rows)[:, None] == fixed_rows[None, :], 1 << 14, chance)
    score = chance * count + jnp.arange(count)
    return lax.top_k(score.astype(jnp.int32), top)[1].astype(jnp.int32)


def bell_draw(own_key, shape, scale, bound, cuts=(), kind=jnp.bfloat16):
    values = jax.random.normal(own_key, shape, jnp.float32) * scale
    if len(cuts) > 0:
        values = steps_of(own_key, shape, cuts, -0.22, 0.18) * values
    return jnp.clip(values, min=-bound, max=bound).astype(kind)


def setup_inputs(seed: int = 0) -> dict:
    splits = jax.random.split(jax.random.key(seed), 7)
    return {
        "source_acts": bell_draw(splits[0], (TOKENS, D), 1.0, 6.0, ((0, 16),)),
        "target_acts": bell_draw(splits[1], (TOKENS, D), 1.0, 6.0, ((0, 16),)),
        "enc_weight": bell_draw(splits[2], (D, F), D ** -0.5, 0.09375, ((1, 48),)),
        "enc_bias": jnp.clip(jax.random.uniform(splits[3], (F,), jnp.float32, -1.0, 1.0) * steps_of(splits[3], (F,), ((0, 48),), -0.4, 0.0), -1.0, 1.0),
        "dec_weight": bell_draw(splits[4], (F, D), (F // 8) ** -0.5, 0.125, ((0, 48),)),
        "active_blocks": distinct(splits[5], (TOKENS // TILE), F // BLOCK, K, 5461),
    }


def smooth_gate(values):
    return jax.nn.gelu(values, approximate=False)

def reference(source_acts, target_acts, enc_weight, enc_bias, dec_weight, active_blocks):
    block_ids = jnp.arange(F // BLOCK, dtype=jnp.int32)
    tile_mask = jnp.any(active_blocks[:, :, None] == block_ids[None, None, :], axis=1).astype(jnp.float32)
    token_mask = jnp.repeat(jnp.repeat(tile_mask, TILE, axis=0), BLOCK, axis=1)
    preact = jnp.dot(source_acts, enc_weight, preferred_element_type=jnp.float32) + enc_bias[None, :]
    gated, slope_fn = jax.vjp(smooth_gate, preact)
    features = (gated * token_mask).astype(jnp.bfloat16)
    recon = jnp.dot(features, dec_weight, preferred_element_type=jnp.float32)
    errors = recon - target_acts.astype(jnp.float32)
    recon_loss = jnp.sum(errors * errors) / (TOKENS * D)
    errors_low = errors.astype(jnp.bfloat16)
    back_prop = jnp.dot(errors_low, dec_weight.T, preferred_element_type=jnp.float32)
    grad_pre = (slope_fn(back_prop)[0] * token_mask).astype(jnp.bfloat16)

    def accumulate(carry, index):
        start = (index * TOK_DEV).astype(jnp.int32)
        x_rows = lax.dynamic_slice_in_dim(source_acts, start, TOK_DEV, 0)
        g_rows = lax.dynamic_slice_in_dim(grad_pre, start, TOK_DEV, 0)
        f_rows = lax.dynamic_slice_in_dim(features, start, TOK_DEV, 0)
        e_rows = lax.dynamic_slice_in_dim(errors_low, start, TOK_DEV, 0)
        enc_term = jnp.dot(x_rows.T, g_rows, preferred_element_type=jnp.float32).astype(jnp.bfloat16)
        dec_term = jnp.dot(f_rows.T, e_rows, preferred_element_type=jnp.float32).astype(jnp.bfloat16)
        enc_term, dec_term = lax.optimization_barrier((enc_term, dec_term))
        return ((carry[0] + enc_term.astype(jnp.float32), carry[1] + dec_term.astype(jnp.float32)), None)
    init = (jnp.zeros((D, F), jnp.float32), jnp.zeros((F, D), jnp.float32))
    totals, unused = lax.scan(accumulate, init, jnp.arange(N_TOK, dtype=jnp.int32))
    return (totals[0], totals[1], recon_loss)
```

```python
import functools
import math

import jax
import jax.numpy as jnp
from jax import lax
from jax.experimental import pallas as pl
from jax.experimental.pallas import tpu as pltpu
from jax.sharding import PartitionSpec as P

BLOCK = 128
TILE = 64
NX = 4
PER_Z = 4
MESH = pl.DeviceIdType.MESH
F32 = jnp.float32
BF16 = jnp.bfloat16


def remote(src, dst, send_sem, recv_sem, device):
    pltpu.make_async_remote_copy(
        src_ref=src, dst_ref=dst, send_sem=send_sem, recv_sem=recv_sem, device_id=device, device_id_type=MESH
    ).start()


def await_bytes(ref, sem):
    pltpu.make_async_copy(ref, ref, sem).wait()


def kernel(dims, src_hbm, tgt_hbm, enc_hbm, bias_ref, dec_hbm, act_ref, genc_ref, gdec_ref, loss_ref, *scratch):
    nt, ny, nz, rows, width, cols, ns = dims
    (src_v, enc_v, dec_v, tgt_v, acc, slope, srcd, fa, ga, err, errd, part, psend, precv, rsend, rrecv, ysend, yrecv, lbuf,
     load_sem, enc_sem, xs_sem, sf_sem, f_send, f_y, f_p, f_m, f_r, g_send, g_y, g_p, g_m, g_r, ps_send, ps_recv,
     rs_send, rs_recv, yh_send, yh_recv, e_zs, e_zp, e_zm, e_sib, d_xs, d_zs, d_zp, d_zm, d_sib, l_sem) = scratch
    half = width // 2
    dblk = width // nt
    chunk = rows // nz
    hrow = rows // 2
    sub_w = half // ns
    n_minus, n_plus = nz // 2, (nz - 1) // 2
    enc_parts = enc_sem.shape[0]
    kpart = width // enc_parts
    n_tiles = ps_recv.shape[0]
    tile_w = half // n_tiles

    t, f = lax.axis_index("tok"), lax.axis_index("feat")
    x, yl = t // ny, t % ny
    z, yh, c = f // PER_Z, (f // 2) % 2, f % 2

    def zmod(v):
        return lax.rem(v + nz, nz)

    def fid(zz, hh, cc):
        return (zz * 2 + hh) * 2 + cc

    def tid(xx, yy):
        return lax.rem(xx + NX, NX) * ny + lax.rem(yy + ny, ny)

    def rows_of(zz):
        return pl.ds(pl.multiple_of(zz * chunk, chunk), chunk)

    def dcols(tt):
        return pl.ds(pl.multiple_of(tt * dblk, dblk), dblk)

    z_up, z_down = (t, fid(zmod(z + 1), yh, c)), (t, fid(zmod(z - 1), yh, c))
    sibling, y_peer = (t, fid(z, yh, 1 - c)), (t, fid(z, 1 - yh, c))
    own_half = pl.ds(pl.multiple_of(hrow * c, hrow), hrow)
    sib_half = pl.ds(pl.multiple_of(hrow * (1 - c), hrow), hrow)
    my_cols = pl.ds(pl.multiple_of(half * c, half), half)
    my_groups = pl.ds(c * (nt // 2), nt // 2)

    def load_enc(k):
        part_rows = pl.ds(k * kpart, kpart)
        return pltpu.make_async_copy(enc_hbm.at[part_rows], enc_v.at[part_rows], enc_sem.at[k])

    loads = [
        pltpu.make_async_copy(src_hbm, src_v, load_sem.at[0]),
        pltpu.make_async_copy(dec_hbm, dec_v, load_sem.at[1]),
        pltpu.make_async_copy(tgt_hbm.at[rows_of(z), my_cols], tgt_v, load_sem.at[2]),
        pltpu.make_async_copy(src_hbm.at[own_half, dcols(t)], srcd.at[t, own_half], load_sem.at[3]),
    ]
    loads[0].start()
    for k in range(enc_parts):
        load_enc(k).start()
    for load in loads[1:]:
        load.start()

    barrier = pltpu.get_barrier_semaphore()
    for k in range(1, nt):
        pl.semaphore_signal(barrier, inc=1, device_id=(lax.rem(t + k, nt), f), device_id_type=MESH)
    for peer in (z_up, z_down, sibling, y_peer):
        pl.semaphore_signal(barrier, inc=1, device_id=peer, device_id_type=MESH)
    pl.semaphore_wait(barrier, nt - 1 + 4)

    for k in range(1, nt):
        to = lax.rem(t + k, nt)
        remote(src_hbm.at[own_half, dcols(to)], srcd.at[t, own_half], xs_sem.at[0], xs_sem.at[1], (to, f))

    loads[0].wait()
    acc[...] = jnp.broadcast_to(bias_ref[...], acc.shape)
    for k in range(enc_parts):
        load_enc(k).wait()
        part_rows = pl.ds(k * kpart, kpart)
        acc[...] += jnp.dot(src_v[:, part_rows], enc_v[part_rows, :], preferred_element_type=F32)

    for tile in range(rows // TILE):
        listed = act_ref[tile : tile + 1, :]
        for blk in range(cols // BLOCK):
            block_id = f * (cols // BLOCK) + blk
            active = jnp.max(jnp.where(listed == block_id, 1.0, 0.0), axis=1, keepdims=True)
            at = (pl.ds(tile * TILE, TILE), pl.ds(blk * BLOCK, BLOCK))
            v = acc[at]
            cdf = 0.5 * (1.0 + lax.erf(v * math.sqrt(0.5)))
            pdf = jnp.exp(-0.5 * v * v) * (1.0 / math.sqrt(2.0 * math.pi))
            fa[t, at[0], at[1]] = (v * cdf * active).astype(BF16)
            slope[at] = (cdf + v * pdf) * active

    def gather_start(buf, send, y_sem, p_sem, m_sem):
        for k in range(1, ny):
            remote(buf.at[t], buf.at[t], send, y_sem.at[k], (tid(x, yl + k), f))
        gather_x(buf, send, p_sem, m_sem, 0)

    def gather_x(buf, send, p_sem, m_sem, k):
        own = tid(x, yl - k)
        remote(buf.at[own], buf.at[own], send, p_sem.at[k], (tid(x + 1, yl), f))
        remote(buf.at[own], buf.at[own], send, m_sem.at[k], (tid(x - 1, yl), f))

    def gather_y(buf, send, y_sem, p_sem, m_sem, k):
        await_bytes(buf.at[tid(x, yl - k)], y_sem.at[k])
        gather_x(buf, send, p_sem, m_sem, k)

    def gather_relay(buf, send, p_sem, m_sem, r_sem, k):
        below, above = tid(x - 1, yl - k), tid(x + 1, yl - k)
        await_bytes(buf.at[below], p_sem.at[k])
        await_bytes(buf.at[above], m_sem.at[k])
        if k < ny // 2:
            remote(buf.at[below], buf.at[below], send, r_sem.at[k], (tid(x + 1, yl), f))
        else:
            remote(buf.at[above], buf.at[above], send, r_sem.at[k], (tid(x - 1, yl), f))

    def gather_far(buf, r_sem, k):
        await_bytes(buf.at[tid(x + 2, yl - k)], r_sem.at[k])

    gather_start(fa, f_send.at[0], f_y, f_p, f_m)

    loads[1].wait()

    @pl.loop(0, n_tiles)
    def _(n):
        at = pl.ds(pl.multiple_of(n * tile_w, tile_w), tile_w)
        full = pl.ds(pl.multiple_of(half * (1 - c) + n * tile_w, tile_w), tile_w)
        psend[:, at] = jnp.dot(fa[t], dec_v[:, full], preferred_element_type=F32).astype(BF16)
        remote(psend.at[:, at], precv.at[:, at], ps_send.at[0], ps_recv.at[n], sibling)

    @pl.loop(0, n_tiles)
    def _(n):
        at = pl.ds(pl.multiple_of(n * tile_w, tile_w), tile_w)
        full = pl.ds(pl.multiple_of(half * c + n * tile_w, tile_w), tile_w)
        part[:, at] = jnp.dot(fa[t], dec_v[:, full], preferred_element_type=F32)

    @pl.loop(0, n_tiles)
    def _(n):
        at = pl.ds(pl.multiple_of(n * tile_w, tile_w), tile_w)
        await_bytes(precv.at[:, at], ps_recv.at[n])
        part[:, at] += precv[:, at].astype(F32)

    def rs_step(slot, prev, owner, sub, device):
        value = part[rows_of(owner), pl.ds(sub * sub_w, sub_w)]
        if prev is not None:
            await_bytes(rrecv.at[prev, sub], rs_recv.at[prev, sub])
            value = value + rrecv[prev, sub].astype(F32)
        rsend[slot, sub] = value.astype(BF16)
        remote(rsend.at[slot, sub], rrecv.at[slot, sub], rs_send.at[0], rs_recv.at[slot, sub], device)

    for s in range(n_minus):
        for sub in range(ns):
            rs_step(s, s - 1 if s else None, zmod(z - (n_minus - s)), sub, z_down)
            if s < n_plus:
                rs_step(n_minus + s, n_minus + s - 1 if s else None, zmod(z + (n_plus - s)), sub, z_up)
    for sub in range(ns):
        value = part[rows_of(z), pl.ds(sub * sub_w, sub_w)]
        for last in (n_minus - 1, n_minus + n_plus - 1):
            await_bytes(rrecv.at[last, sub], rs_recv.at[last, sub])
            value = value + rrecv[last, sub].astype(F32)
        ysend[sub] = value.astype(BF16)
        remote(ysend.at[sub], yrecv.at[sub], yh_send.at[0], yh_recv.at[sub], y_peer)

    for sub in range(ns):
        await_bytes(yrecv.at[sub], yh_recv.at[sub])
        recon = ysend[sub].astype(F32) + yrecv[sub].astype(F32)
        target = tgt_v[:, pl.ds(sub * sub_w, sub_w)] if sub else None
        if sub == 0:
            loads[2].wait()
            target = tgt_v[:, pl.ds(0, sub_w)]
        at = pl.ds(pl.multiple_of(half * c + sub * sub_w, sub_w), sub_w)
        err[rows_of(z), at] = (recon - target.astype(F32)).astype(BF16)

    def ring_send(piece, send, p_sem, m_sem, up, down, own):
        if up is not None:
            remote(piece, piece, send, p_sem.at[up], z_up)
        if down is not None:
            remote(piece, piece, send, m_sem.at[down], z_down)
        remote(piece, piece, own[0], own[1], sibling)

    def ring(piece_of, send, p_sem, m_sem, sib_send, sib_own, sib_recv, between):
        ring_send(piece_of(z), send, p_sem, m_sem, 0, 0 if n_plus else None, (sib_send, sib_own))
        for s in range(1, n_minus + 1):
            piece = piece_of(zmod(z - s))
            await_bytes(piece, p_sem.at[s - 1])
            ring_send(piece, send, p_sem, m_sem, s if s < n_minus else None, None, (sib_send, sib_recv))
            if s <= n_plus:
                piece = piece_of(zmod(z + s))
                await_bytes(piece, m_sem.at[s - 1])
                ring_send(piece, send, p_sem, m_sem, None, s if s < n_plus else None, (sib_send, sib_recv))
            between(s)

    def err_piece(zz):
        return err.at[rows_of(zz), my_cols]

    mine = t // (nt // 2) == c

    def between_err(s):
        if s == 1:
            await_bytes(err_piece(z), e_sib.at[1])

            @pl.when(mine)
            def _():
                for k in range(1, nt):
                    to = lax.rem(t + k, nt)
                    remote(err.at[rows_of(z), dcols(to)], errd.at[t, z], d_xs.at[0], d_xs.at[1], (to, f))
                errd[t, z] = err[rows_of(z), dcols(t)]
        if s == 2:
            for k in range(1, ny):
                gather_y(fa, f_send.at[0], f_y, f_p, f_m, k)

    ring(err_piece, e_zs.at[0], e_zp, e_zm, e_sib.at[0], e_sib.at[1], e_sib.at[2], between_err)
    await_bytes(err.at[pl.ds(0, rows - chunk), pl.ds(0, half)], e_sib.at[2])

    acc[...] = jnp.zeros_like(acc)

    @pl.loop(0, enc_parts)
    def _(k):
        at = pl.ds(pl.multiple_of(k * kpart, kpart), kpart)
        acc[...] += lax.dot_general(err[:, at], dec_v[:, at], (((1,), (1,)), ((), ())), preferred_element_type=F32)

    ga[t] = (acc[...] * slope[...]).astype(BF16)
    gather_start(ga, g_send.at[0], g_y, g_p, g_m)

    total = jnp.zeros((16, 128), F32)
    for k in range(width // 128):
        piece = err[:, pl.ds(k * 128, 128)].astype(F32)
        piece = piece * piece
        for r in range(rows // 16):
            total = total + piece[r * 16 : (r + 1) * 16]
    lbuf[t] = total[:8] + total[8:]
    for k in range(1, nt):
        remote(lbuf.at[t], lbuf.at[t], l_sem.at[0], l_sem.at[1], (lax.rem(t + k, nt), f))

    def errd_piece(zz):
        return errd.at[my_groups, zz]

    @pl.when(mine)
    def _():
        await_bytes(errd.at[pl.ds(0, nt // 2 - 1), 0], d_xs.at[1])

    @pl.when(jnp.logical_not(mine))
    def _():
        await_bytes(errd.at[pl.ds(0, nt // 2), 0], d_xs.at[1])

    def between_errd(s):
        if s == 1:
            loads[3].wait()
            await_bytes(srcd.at[pl.ds(0, nt - 1), pl.ds(0, hrow)], xs_sem.at[1])
            remote(srcd.at[:, own_half], srcd.at[:, own_half], sf_sem.at[0], sf_sem.at[1], sibling)
            for k in range(ny):
                gather_relay(fa, f_send.at[0], f_p, f_m, f_r, k)
        if 2 <= s <= ny:
            gather_y(ga, g_send.at[0], g_y, g_p, g_m, s - 1)

    ring(errd_piece, d_zs.at[0], d_zp, d_zm, d_sib.at[0], d_sib.at[1], d_sib.at[1], between_errd)
    for k in range(n_minus + 1, ny + 1):
        between_errd(k)
    for k in range(ny):
        gather_relay(ga, g_send.at[0], g_p, g_m, g_r, k)
    for k in range(ny):
        gather_far(fa, f_r, k)
    await_bytes(errd.at[pl.ds(0, nt // 2)], d_sib.at[1])
    await_bytes(srcd.at[:, sib_half], sf_sem.at[1])

    across = (((0,), (0,)), ((), ()))
    gdec_ref[...] = jnp.zeros_like(gdec_ref)

    @pl.loop(0, nt)
    def _(g):
        gdec_ref[...] += lax.dot_general(fa[g], errd[g].reshape(rows, dblk), across, preferred_element_type=F32)

    genc_ref[...] = jnp.zeros_like(genc_ref)

    def enc_group(g):
        genc_ref[...] += lax.dot_general(srcd[g], ga[g], across, preferred_element_type=F32)

    @pl.loop(0, (NX - 1) * ny)
    def _(n):
        dx = n // ny
        enc_group(tid(x + jnp.where(dx == 2, NX - 1, dx), yl - n % ny))

    for k in range(ny):
        gather_far(ga, g_r, k)

    @pl.loop(0, ny)
    def _(k):
        enc_group(tid(x + 2, yl - k))

    await_bytes(lbuf.at[pl.ds(0, nt - 1)], l_sem.at[1])
    sums = lbuf[0]
    for k in range(1, nt):
        sums = sums + lbuf[k]
    loss_ref[0, 0] = jnp.sum(sums) / (rows * nt * width)

    await_bytes(srcd.at[pl.ds(0, nt - 1), pl.ds(0, hrow)], xs_sem.at[0])
    await_bytes(srcd.at[:, own_half], sf_sem.at[0])
    await_bytes(fa.at[pl.ds(0, nt - 1)], f_send.at[0])
    await_bytes(ga.at[pl.ds(0, nt - 1)], g_send.at[0])
    await_bytes(psend, ps_send.at[0])
    await_bytes(rsend, rs_send.at[0])
    await_bytes(ysend, yh_send.at[0])
    await_bytes(err.at[pl.ds(0, rows - chunk), pl.ds(0, half)], e_zs.at[0])
    await_bytes(err.at[:, pl.ds(0, half)], e_sib.at[0])
    await_bytes(errd.at[pl.ds(0, nt // 2), pl.ds(0, nz - 1)], d_zs.at[0])
    await_bytes(errd.at[pl.ds(0, nt // 2)], d_sib.at[0])
    await_bytes(lbuf.at[pl.ds(0, nt - 1)], l_sem.at[0])

    @pl.when(mine)
    def _():
        await_bytes(errd.at[pl.ds(0, nt - 1), 0], d_xs.at[0])


def on_device(nt, nf, ns, source_acts, target_acts, enc_weight, enc_bias, dec_weight, active_blocks):
    rows, width = source_acts.shape
    cols = enc_weight.shape[1]
    ny, nz = nt // NX, nf // PER_Z
    half, dblk, chunk = width // 2, width // nt, rows // nz
    enc_parts, n_tiles = 4, 4
    n_minus, n_plus = nz // 2, (nz - 1) // 2
    dma = lambda *shape: pltpu.SemaphoreType.DMA(shape)
    scratch = [
        pltpu.VMEM((rows, width), BF16),
        pltpu.VMEM((width, cols), BF16),
        pltpu.VMEM((cols, width), BF16),
        pltpu.VMEM((chunk, half), BF16),
        pltpu.VMEM((rows, cols), F32),
        pltpu.VMEM((rows, cols), F32),
        pltpu.VMEM((nt, rows, dblk), BF16),
        pltpu.VMEM((nt, rows, cols), BF16),
        pltpu.VMEM((nt, rows, cols), BF16),
        pltpu.VMEM((rows, width), BF16),
        pltpu.VMEM((nt, nz, chunk, dblk), BF16),
        pltpu.VMEM((rows, half), F32),
        pltpu.VMEM((rows, half), BF16),
        pltpu.VMEM((rows, half), BF16),
        pltpu.VMEM((nz - 1, ns, chunk, half // ns), BF16),
        pltpu.VMEM((nz - 1, ns, chunk, half // ns), BF16),
        pltpu.VMEM((ns, chunk, half // ns), BF16),
        pltpu.VMEM((ns, chunk, half // ns), BF16),
        pltpu.VMEM((nt, 8, 128), F32),
        dma(4), dma(enc_parts), dma(2), dma(2),
        dma(1), dma(ny), dma(ny), dma(ny), dma(ny),
        dma(1), dma(ny), dma(ny), dma(ny), dma(ny),
        dma(1), dma(n_tiles),
        dma(1), dma(nz - 1, ns), dma(1), dma(ns),
        dma(1), dma(n_minus), dma(max(n_plus, 1)), dma(3),
        dma(2), dma(1), dma(n_minus), dma(max(n_plus, 1)), dma(2),
        dma(2),
    ]
    vmem = pl.BlockSpec(memory_space=pltpu.VMEM)
    hbm = pl.BlockSpec(memory_space=pl.ANY)
    grad_encoder, grad_decoder, loss = pl.pallas_call(
        functools.partial(kernel, (nt, ny, nz, rows, width, cols, ns)),
        out_shape=(
            jax.ShapeDtypeStruct((dblk, cols), F32),
            jax.ShapeDtypeStruct((cols, dblk), F32),
            jax.ShapeDtypeStruct((1, 1), F32),
        ),
        in_specs=[hbm, hbm, hbm, vmem, hbm, vmem],
        out_specs=(vmem, vmem, pl.BlockSpec(memory_space=pltpu.SMEM)),
        scratch_shapes=scratch,
        compiler_params=pltpu.CompilerParams(
            collective_id=0, has_side_effects=True, vmem_limit_bytes=48 * 1024 * 1024
        ),
        name="step",
    )(source_acts, target_acts, enc_weight, enc_bias.reshape(1, cols), dec_weight, active_blocks)
    return grad_encoder, grad_decoder, loss.reshape(())


def solution(mesh):
    placed = (
        P("tok", None),
        P("tok", None),
        P(None, "feat"),
        P("feat"),
        P("feat", None),
        P("tok", None),
    )
    return jax.shard_map(
        functools.partial(on_device, mesh.shape["tok"], mesh.shape["feat"], 2),
        mesh=mesh,
        in_specs=placed,
        out_specs=(P("tok", "feat"), P("feat", "tok"), P()),
        check_vma=False,
    )
```

```python
import functools
import math

import jax
import jax.numpy as jnp
from jax import lax
from jax.experimental import pallas as pl
from jax.experimental.pallas import tpu as pltpu
from jax.sharding import PartitionSpec as P

BLOCK = 128
TILE = 64
NX = 4
PER_Z = 4
MESH = pl.DeviceIdType.MESH
F32 = jnp.float32
BF16 = jnp.bfloat16


def remote(src, dst, send_sem, recv_sem, device):
    pltpu.make_async_remote_copy(
        src_ref=src, dst_ref=dst, send_sem=send_sem, recv_sem=recv_sem, device_id=device, device_id_type=MESH
    ).start()


def await_bytes(ref, sem):
    pltpu.make_async_copy(ref, ref, sem).wait()


def kernel(dims, src_hbm, tgt_hbm, enc_hbm, bias_hbm, dec_hbm, act_hbm, genc_ref, gdec_ref, loss_ref, *scratch):
    nt, ny, nz, rows, width, cols, ns, e_subs = dims
    (src_v, enc_v, dec_v, bias_ref, act_ref, tgt_v, acc, slope, srcd, fa, ga, err, errd, part, psend, precv, rsend, rrecv, ysend, yrecv, lbuf, lpart,
     load_sem, enc_sem, xs_sem, sf_sem, f_send, f_y, f_p, f_m, f_r, g_send, g_y, g_p, g_m, g_r, ps_send, ps_recv,
     rs_send, rs_recv, yh_send, yh_recv, e_zs, e_zp, e_zm, e_sib, d_xs, d_zs, d_zp, d_zm, d_sib, l_sem) = scratch
    half = width // 2
    dblk = width // nt
    chunk = rows // nz
    hrow = rows // 2
    sub_w = half // ns
    n_minus, n_plus = nz // 2, (nz - 1) // 2
    enc_parts = enc_sem.shape[0]
    kpart = width // enc_parts
    n_tiles = ps_recv.shape[0]
    tile_w = half // n_tiles

    t, f = lax.axis_index("tok"), lax.axis_index("feat")
    x, yl = t // ny, t % ny
    z, yh, c = f // PER_Z, (f // 2) % 2, f % 2

    def zmod(v):
        return lax.rem(v + nz, nz)

    def fid(zz, hh, cc):
        return (zz * 2 + hh) * 2 + cc

    def tid(xx, yy):
        return lax.rem(xx + NX, NX) * ny + lax.rem(yy + ny, ny)

    def rows_of(zz):
        return pl.ds(pl.multiple_of(zz * chunk, chunk), chunk)

    def dcols(tt):
        return pl.ds(pl.multiple_of(tt * dblk, dblk), dblk)

    z_up, z_down = (t, fid(zmod(z + 1), yh, c)), (t, fid(zmod(z - 1), yh, c))
    sibling, y_peer = (t, fid(z, yh, 1 - c)), (t, fid(z, 1 - yh, c))
    own_half = pl.ds(pl.multiple_of(hrow * c, hrow), hrow)
    sib_half = pl.ds(pl.multiple_of(hrow * (1 - c), hrow), hrow)
    my_cols = pl.ds(pl.multiple_of(half * c, half), half)
    my_groups = pl.ds(c * (nt // 2), nt // 2)

    def load_enc(k):
        part_rows = pl.ds(k * kpart, kpart)
        return pltpu.make_async_copy(enc_hbm.at[part_rows], enc_v.at[part_rows], enc_sem.at[k])

    loads = [
        pltpu.make_async_copy(src_hbm, src_v, load_sem.at[0]),
        pltpu.make_async_copy(dec_hbm, dec_v, load_sem.at[1]),
        pltpu.make_async_copy(tgt_hbm.at[rows_of(z), my_cols], tgt_v, load_sem.at[2]),
        pltpu.make_async_copy(src_hbm.at[own_half, dcols(t)], srcd.at[t, own_half], load_sem.at[3]),
        pltpu.make_async_copy(bias_hbm, bias_ref, load_sem.at[4]),
        pltpu.make_async_copy(act_hbm, act_ref, load_sem.at[5]),
    ]
    loads[0].start()
    for k in range(enc_parts):
        load_enc(k).start()
    for load in loads[1:]:
        load.start()

    barrier = pltpu.get_barrier_semaphore()
    for k in range(1, nt):
        pl.semaphore_signal(barrier, inc=1, device_id=(lax.rem(t + k, nt), f), device_id_type=MESH)
    for peer in (z_up, z_down, sibling, y_peer):
        pl.semaphore_signal(barrier, inc=1, device_id=peer, device_id_type=MESH)
    pl.semaphore_wait(barrier, nt - 1 + 4)

    for load in (loads[0], loads[4], loads[5]):
        load.wait()
    acc[...] = jnp.broadcast_to(bias_ref[...][None, :], acc.shape)
    for k in range(enc_parts):
        load_enc(k).wait()
        part_rows = pl.ds(k * kpart, kpart)
        acc[...] += jnp.dot(src_v[:, part_rows], enc_v[part_rows, :], preferred_element_type=F32)

    for tile in range(rows // TILE):
        listed = act_ref[tile : tile + 1, :]
        for blk in range(cols // BLOCK):
            block_id = f * (cols // BLOCK) + blk
            active = jnp.max(jnp.where(listed == block_id, 1.0, 0.0), axis=1, keepdims=True)
            at = (pl.ds(tile * TILE, TILE), pl.ds(blk * BLOCK, BLOCK))
            v = acc[at]
            cdf = 0.5 * (1.0 + lax.erf(v * math.sqrt(0.5)))
            pdf = jnp.exp(-0.5 * v * v) * (1.0 / math.sqrt(2.0 * math.pi))
            fa[t, at[0], at[1]] = (v * cdf * active).astype(BF16)
            slope[at] = (cdf + v * pdf) * active

    def gather_start(part, send, y_sem, p_sem, m_sem):
        for k in range(1, ny):
            remote(part(t), part(t), send, y_sem.at[k], (tid(x, yl + k), f))
        gather_x(part, send, p_sem, m_sem, 0)

    def gather_x(part, send, p_sem, m_sem, k):
        own = part(tid(x, yl - k))
        remote(own, own, send, p_sem.at[k], (tid(x + 1, yl), f))
        remote(own, own, send, m_sem.at[k], (tid(x - 1, yl), f))

    def gather_y(part, send, y_sem, p_sem, m_sem):
        for k in range(1, ny):
            await_bytes(part(tid(x, yl - k)), y_sem.at[k])
            gather_x(part, send, p_sem, m_sem, k)

    def gather_relay(part, send, p_sem, m_sem, r_sem):
        for k in range(ny):
            below, above = part(tid(x - 1, yl - k)), part(tid(x + 1, yl - k))
            if k < ny // 2:
                await_bytes(below, p_sem.at[k])
                remote(below, below, send, r_sem.at[k], (tid(x + 1, yl), f))
                await_bytes(above, m_sem.at[k])
            else:
                await_bytes(above, m_sem.at[k])
                remote(above, above, send, r_sem.at[k], (tid(x - 1, yl), f))
                await_bytes(below, p_sem.at[k])

    def gather_far(part, r_sem):
        for k in range(ny):
            await_bytes(part(tid(x + 2, yl - k)), r_sem.at[k])

    near = max(1, n_minus // 2)
    n_early = 2 * near + 1
    cuts = (pl.ds(0, n_early * chunk), pl.ds(n_early * chunk, rows - n_early * chunk))

    def features_of(g):
        return fa.at[g]

    def grads_of(h):
        return lambda g: ga.at[g, cuts[h]]

    gather_start(features_of, f_send.at[0], f_y, f_p, f_m)

    for k in range(1, nt):
        to = lax.rem(t + k, nt)
        remote(src_hbm.at[own_half, dcols(to)], srcd.at[t, own_half], xs_sem.at[0], xs_sem.at[1], (to, f))

    loads[1].wait()

    @pl.loop(0, n_tiles)
    def _(n):
        at = pl.ds(pl.multiple_of(n * tile_w, tile_w), tile_w)
        full = pl.ds(pl.multiple_of(half * (1 - c) + n * tile_w, tile_w), tile_w)
        psend[:, at] = jnp.dot(fa[t], dec_v[:, full], preferred_element_type=F32).astype(BF16)
        remote(psend.at[:, at], precv.at[:, at], ps_send.at[0], ps_recv.at[n], sibling)

    @pl.loop(0, n_tiles)
    def _(n):
        at = pl.ds(pl.multiple_of(n * tile_w, tile_w), tile_w)
        full = pl.ds(pl.multiple_of(half * c + n * tile_w, tile_w), tile_w)
        part[:, at] = jnp.dot(fa[t], dec_v[:, full], preferred_element_type=F32)

    @pl.loop(0, n_tiles)
    def _(n):
        at = pl.ds(pl.multiple_of(n * tile_w, tile_w), tile_w)
        await_bytes(precv.at[:, at], ps_recv.at[n])
        part[:, at] += precv[:, at].astype(F32)

    def rs_step(slot, prev, owner, sub, device):
        value = part[rows_of(owner), pl.ds(sub * sub_w, sub_w)]
        if prev is not None:
            await_bytes(rrecv.at[prev, sub], rs_recv.at[prev, sub])
            value = value + rrecv[prev, sub].astype(F32)
        rsend[slot, sub] = value.astype(BF16)
        remote(rsend.at[slot, sub], rrecv.at[slot, sub], rs_send.at[0], rs_recv.at[slot, sub], device)

    for s in range(n_minus):
        for sub in range(ns):
            rs_step(s, s - 1 if s else None, zmod(z - (n_minus - s)), sub, z_down)
            if s < n_plus:
                rs_step(n_minus + s, n_minus + s - 1 if s else None, zmod(z + (n_plus - s)), sub, z_up)
    for sub in range(ns):
        value = part[rows_of(z), pl.ds(sub * sub_w, sub_w)]
        for last in (n_minus - 1, n_minus + n_plus - 1):
            await_bytes(rrecv.at[last, sub], rs_recv.at[last, sub])
            value = value + rrecv[last, sub].astype(F32)
        ysend[sub] = value.astype(BF16)
        remote(ysend.at[sub], yrecv.at[sub], yh_send.at[0], yh_recv.at[sub], y_peer)

    own_rows = pl.ds(near * chunk, chunk)
    gather_y(features_of, f_send.at[0], f_y, f_p, f_m)
    for sub in range(ns):
        await_bytes(yrecv.at[sub], yh_recv.at[sub])
        recon = ysend[sub].astype(F32) + yrecv[sub].astype(F32)
        target = tgt_v[:, pl.ds(sub * sub_w, sub_w)] if sub else None
        if sub == 0:
            loads[2].wait()
            target = tgt_v[:, pl.ds(0, sub_w)]
        at = pl.ds(pl.multiple_of(half * c + sub * sub_w, sub_w), sub_w)
        err[own_rows, at] = (recon - target.astype(F32)).astype(BF16)

    def ring_start(piece_of, next_of, subs, send, p_sem, m_sem, sib_send, sib_recv):
        for sub in range(subs):
            piece = piece_of(0, sub)
            remote(piece, piece, sib_send, sib_recv, sibling)
            remote(piece, next_of(0, -1, sub), send, p_sem.at[0, sub], z_up)
            remote(piece, next_of(0, 1, sub), send, m_sem.at[0, sub], z_down)

    def ring_step(piece_of, next_of, subs, s, send, p_sem, m_sem, sib_send, sib_recv):
        arrived = []
        for sub in range(subs):
            for sem, sign, hops, device in ((p_sem, -1, n_minus, z_up), (m_sem, 1, n_plus, z_down)):
                if s <= hops:
                    piece = piece_of(sign * s, sub)
                    await_bytes(piece, sem.at[s - 1, sub])
                    if s < hops:
                        remote(piece, next_of(sign * s, sign, sub), send, sem.at[s, sub], device)
                    arrived.append(piece)
        for piece in arrived:
            remote(piece, piece, sib_send, sib_recv, sibling)

    err_w = half // e_subs

    def err_piece(hop, sub):
        at = pl.ds((near + hop) % nz * chunk, chunk)
        return err.at[at, pl.ds(pl.multiple_of(half * c + err_w * sub, err_w), err_w)]

    def err_next(hop, sign, sub):
        return err_piece(hop + sign, sub)

    def errd_piece(hop, sub):
        return errd.at[my_groups, zmod(z + hop)]

    def errd_next(hop, sign, sub):
        return errd_piece(hop, sub)

    e_ring = (e_zs.at[0], e_zp, e_zm, e_sib.at[0])
    d_ring = (d_zs.at[0], d_zp, d_zm, d_sib.at[0], d_sib.at[1])
    mine = t // (nt // 2) == c

    def errd_send():
        await_bytes(err.at[own_rows, my_cols], e_sib.at[1])

        @pl.when(mine)
        def _():
            for k in range(1, nt):
                to = lax.rem(t + k, nt)
                remote(err.at[own_rows, dcols(to)], errd.at[t, z], d_xs.at[0], d_xs.at[1], (to, f))
            errd[t, z] = err[own_rows, dcols(t)]

    def errd_start():
        @pl.when(mine)
        def _():
            await_bytes(errd.at[pl.ds(0, nt // 2 - 1), 0], d_xs.at[1])

        @pl.when(jnp.logical_not(mine))
        def _():
            await_bytes(errd.at[pl.ds(0, nt // 2), 0], d_xs.at[1])

        ring_start(errd_piece, errd_next, 1, *d_ring)

    def errd_step(s):
        ring_step(errd_piece, errd_next, 1, s, *d_ring)

    def rows_at(place):
        return rows_of(zmod(z + place - near))

    def back(h):
        acc[cuts[h], :] = jnp.zeros((cuts[h].size, cols), F32)

        @pl.loop(0, enc_parts)
        def _(k):
            at = pl.ds(pl.multiple_of(k * kpart, kpart), kpart)
            acc[cuts[h], :] += lax.dot_general(
                err[cuts[h], at], dec_v[:, at], (((1,), (1,)), ((), ())), preferred_element_type=F32
            )

        for place in range(cuts[h].start // chunk, (cuts[h].start + cuts[h].size) // chunk):
            at = pl.ds(place * chunk, chunk)
            ga[t, at, :] = (acc[at, :] * slope[rows_at(place), :]).astype(BF16)
        gather_start(grads_of(h), g_send.at[h], g_y.at[h], g_p.at[h], g_m.at[h])

    ring_start(err_piece, err_next, e_subs, *e_ring, e_sib.at[1])
    d_lag = near
    for s in range(1, n_minus + 1):
        ring_step(err_piece, err_next, e_subs, s, *e_ring, e_sib.at[2 if s <= near else 3])
        if s == 1:
            errd_send()
        if s == 2:
            loads[3].wait()
            await_bytes(srcd.at[pl.ds(0, nt - 1), pl.ds(0, hrow)], xs_sem.at[1])
            remote(srcd.at[:, own_half], srcd.at[:, own_half], sf_sem.at[0], sf_sem.at[1], sibling)
        if s == 3:
            gather_relay(features_of, f_send.at[0], f_p, f_m, f_r)
        if s == d_lag:
            errd_start()
        if s > d_lag:
            errd_step(s - d_lag)
        if s == near + 1:
            await_bytes(err.at[pl.ds(0, (n_early - 1) * chunk), pl.ds(0, half)], e_sib.at[2])
            back(0)
    await_bytes(err.at[pl.ds(0, rows - n_early * chunk), pl.ds(0, half)], e_sib.at[3])
    back(1)

    errd_step(n_minus - d_lag + 1)
    gather_y(grads_of(0), g_send.at[0], g_y.at[0], g_p.at[0], g_m.at[0])

    for place in range(nz):
        total = jnp.zeros((16, 128), F32)
        for r in range(chunk // 16):
            for k in range(width // 128):
                piece = err[pl.ds(place * chunk + r * 16, 16), pl.ds(k * 128, 128)].astype(F32)
                total = total + piece * piece
        lpart[zmod(z + place - near)] = total[:8] + total[8:]
    total = lpart[0]
    for k in range(1, nz):
        total = total + lpart[k]
    lbuf[t] = total
    for k in range(1, nt):
        remote(lbuf.at[t], lbuf.at[t], l_sem.at[0], l_sem.at[1], (lax.rem(t + k, nt), f))

    if n_minus - d_lag + 2 <= n_minus:
        errd_step(n_minus - d_lag + 2)
    gather_y(grads_of(1), g_send.at[1], g_y.at[1], g_p.at[1], g_m.at[1])
    gather_relay(grads_of(0), g_send.at[0], g_p.at[0], g_m.at[0], g_r.at[0])
    for s in range(n_minus - d_lag + 3, n_minus + 1):
        errd_step(s)

    across = (((0,), (0,)), ((), ()))
    genc_ref[...] = jnp.zeros_like(genc_ref)
    gdec_ref[...] = jnp.zeros_like(gdec_ref)

    def enc_groups(dx):
        @pl.loop(0, ny)
        def _(k):
            g = tid(x + dx, yl - k)
            source = jnp.concatenate([srcd[g, rows_at(place), :] for place in range(nz)], axis=0)
            genc_ref[...] += lax.dot_general(source, ga[g], across, preferred_element_type=F32)

    def dec_groups(first):
        @pl.loop(first, first + nt // 2)
        def _(g):
            gdec_ref[...] += lax.dot_general(fa[g], errd[g].reshape(rows, dblk), across, preferred_element_type=F32)

    await_bytes(srcd.at[:, sib_half], sf_sem.at[1])
    enc_groups(0)
    gather_relay(grads_of(1), g_send.at[1], g_p.at[1], g_m.at[1], g_r.at[1])
    gather_far(features_of, f_r)
    await_bytes(errd.at[pl.ds(0, nt // 2)], d_sib.at[1])
    dec_groups(0)
    dec_groups(nt // 2)
    enc_groups(1)
    enc_groups(-1)
    await_bytes(lbuf.at[pl.ds(0, nt - 1)], l_sem.at[1])
    sums = lbuf[0]
    for k in range(1, nt):
        sums = sums + lbuf[k]
    loss_ref[0, 0] = jnp.sum(sums) / (rows * nt * width)
    gather_far(grads_of(0), g_r.at[0])
    gather_far(grads_of(1), g_r.at[1])
    enc_groups(2)

    await_bytes(srcd.at[pl.ds(0, nt - 1), pl.ds(0, hrow)], xs_sem.at[0])
    await_bytes(srcd.at[:, own_half], sf_sem.at[0])
    await_bytes(fa.at[pl.ds(0, nt - 1)], f_send.at[0])
    for h in range(2):
        await_bytes(ga.at[pl.ds(0, nt - 1), cuts[h]], g_send.at[h])
    await_bytes(psend, ps_send.at[0])
    await_bytes(rsend, rs_send.at[0])
    await_bytes(ysend, yh_send.at[0])
    await_bytes(err.at[pl.ds(0, rows - chunk), pl.ds(0, half)], e_zs.at[0])
    await_bytes(err.at[:, pl.ds(0, half)], e_sib.at[0])
    await_bytes(errd.at[pl.ds(0, nt // 2), pl.ds(0, nz - 1)], d_zs.at[0])
    await_bytes(errd.at[pl.ds(0, nt // 2)], d_sib.at[0])
    await_bytes(lbuf.at[pl.ds(0, nt - 1)], l_sem.at[0])

    @pl.when(mine)
    def _():
        await_bytes(errd.at[pl.ds(0, nt - 1), 0], d_xs.at[0])


def on_device(nt, nf, ns, e_subs, source_acts, target_acts, enc_weight, enc_bias, dec_weight, active_blocks):
    rows, width = source_acts.shape
    cols = enc_weight.shape[1]
    ny, nz = nt // NX, nf // PER_Z
    half, dblk, chunk = width // 2, width // nt, rows // nz
    enc_parts, n_tiles = 4, 4
    n_minus, n_plus = nz // 2, (nz - 1) // 2
    dma = lambda *shape: pltpu.SemaphoreType.DMA(shape)
    scratch = [
        pltpu.VMEM((rows, width), BF16),
        pltpu.VMEM((width, cols), BF16),
        pltpu.VMEM((cols, width), BF16),
        pltpu.VMEM((cols,), F32),
        pltpu.VMEM(active_blocks.shape, jnp.int32),
        pltpu.VMEM((chunk, half), BF16),
        pltpu.VMEM((rows, cols), F32),
        pltpu.VMEM((rows, cols), F32),
        pltpu.VMEM((nt, rows, dblk), BF16),
        pltpu.VMEM((nt, rows, cols), BF16),
        pltpu.VMEM((nt, rows, cols), BF16),
        pltpu.VMEM((rows, width), BF16),
        pltpu.VMEM((nt, nz, chunk, dblk), BF16),
        pltpu.VMEM((rows, half), F32),
        pltpu.VMEM((rows, half), BF16),
        pltpu.VMEM((rows, half), BF16),
        pltpu.VMEM((nz - 1, ns, chunk, half // ns), BF16),
        pltpu.VMEM((nz - 1, ns, chunk, half // ns), BF16),
        pltpu.VMEM((ns, chunk, half // ns), BF16),
        pltpu.VMEM((ns, chunk, half // ns), BF16),
        pltpu.VMEM((nt, 8, 128), F32),
        pltpu.VMEM((nz, 8, 128), F32),
        dma(6), dma(enc_parts), dma(2), dma(2),
        dma(1), dma(ny), dma(ny), dma(ny), dma(ny),
        dma(2), dma(2, ny), dma(2, ny), dma(2, ny), dma(2, ny),
        dma(1), dma(n_tiles),
        dma(1), dma(nz - 1, ns), dma(1), dma(ns),
        dma(1), dma(n_minus, e_subs), dma(n_plus, e_subs), dma(4),
        dma(2), dma(1), dma(n_minus, 1), dma(n_plus, 1), dma(2),
        dma(2),
    ]
    vmem = pl.BlockSpec(memory_space=pltpu.VMEM)
    hbm = pl.BlockSpec(memory_space=pltpu.HBM)
    grad_encoder, grad_decoder, loss = pl.pallas_call(
        functools.partial(kernel, (nt, ny, nz, rows, width, cols, ns, e_subs)),
        out_shape=(
            jax.ShapeDtypeStruct((dblk, cols), F32),
            jax.ShapeDtypeStruct((cols, dblk), F32),
            jax.ShapeDtypeStruct((1, 1), F32),
        ),
        in_specs=[hbm] * 6,
        out_specs=(vmem, vmem, pl.BlockSpec(memory_space=pltpu.SMEM)),
        scratch_shapes=scratch,
        compiler_params=pltpu.CompilerParams(
            collective_id=0, has_side_effects=True, vmem_limit_bytes=60 * 1024 * 1024
        ),
        name="step",
    )(source_acts, target_acts, enc_weight, enc_bias, dec_weight, active_blocks)
    return grad_encoder, grad_decoder, loss.reshape(())


def solution(mesh):
    placed = (
        P("tok", None),
        P("tok", None),
        P(None, "feat"),
        P("feat"),
        P("feat", None),
        P("tok", None),
    )
    return jax.shard_map(
        functools.partial(on_device, mesh.shape["tok"], mesh.shape["feat"], 2, 2),
        mesh=mesh,
        in_specs=placed,
        out_specs=(P("tok", "feat"), P("feat", "tok"), P()),
        check_vma=False,
    )
```

```python
import functools
import math

import jax
import jax.numpy as jnp
from jax import lax
from jax.experimental import pallas as pl
from jax.experimental.pallas import tpu as pltpu
from jax.sharding import PartitionSpec as P

BLOCK = 128
TILE = 64
NX = 4
PER_Z = 4
MESH = pl.DeviceIdType.MESH
F32 = jnp.float32
BF16 = jnp.bfloat16


def remote(src, dst, send_sem, recv_sem, device):
    pltpu.make_async_remote_copy(
        src_ref=src, dst_ref=dst, send_sem=send_sem, recv_sem=recv_sem, device_id=device, device_id_type=MESH
    ).start()


def await_bytes(ref, sem):
    pltpu.make_async_copy(ref, ref, sem).wait()


def kernel(dims, src_hbm, tgt_hbm, enc_hbm, bias_hbm, dec_hbm, act_hbm, genc_ref, gdec_ref, loss_ref, *scratch):
    nt, ny, nz, rows, width, cols, ns, e_subs = dims
    (src_v, enc_v, dec_v, bias_ref, act_ref, tgt_v, acc, slope, srcd, fa, ga, err, errd, part, psend, precv, rsend, rrecv, ysend, yrecv, lbuf, lpart,
     load_sem, enc_sem, xs_sem, sf_sem, f_send, f_y, f_p, f_m, f_r, g_send, g_y, g_p, g_m, g_r, g_all, ps_send, ps_recv,
     rs_send, rs_recv, yh_send, yh_recv, e_zs, e_zp, e_zm, e_sib, d_xs, d_zs, d_zp, d_zm, d_sib, l_sem) = scratch
    half = width // 2
    dblk = width // nt
    chunk = rows // nz
    hrow = rows // 2
    sub_w = half // ns
    n_minus, n_plus = nz // 2, (nz - 1) // 2
    enc_parts = enc_sem.shape[0]
    kpart = width // enc_parts
    n_tiles = ps_recv.shape[0]
    tile_w = half // n_tiles

    t, f = lax.axis_index("tok"), lax.axis_index("feat")
    x, yl = t // ny, t % ny
    z, yh, c = f // PER_Z, (f // 2) % 2, f % 2

    def zmod(v):
        return lax.rem(v + nz, nz)

    def fid(zz, hh, cc):
        return (zz * 2 + hh) * 2 + cc

    def tid(xx, yy):
        return lax.rem(xx + NX, NX) * ny + lax.rem(yy + ny, ny)

    def rows_of(zz):
        return pl.ds(pl.multiple_of(zz * chunk, chunk), chunk)

    def dcols(tt):
        return pl.ds(pl.multiple_of(tt * dblk, dblk), dblk)

    z_up, z_down = (t, fid(zmod(z + 1), yh, c)), (t, fid(zmod(z - 1), yh, c))
    sibling, y_peer = (t, fid(z, yh, 1 - c)), (t, fid(z, 1 - yh, c))
    own_half = pl.ds(pl.multiple_of(hrow * c, hrow), hrow)
    sib_half = pl.ds(pl.multiple_of(hrow * (1 - c), hrow), hrow)
    my_cols = pl.ds(pl.multiple_of(half * c, half), half)
    my_groups = pl.ds(c * (nt // 2), nt // 2)

    def load_enc(k):
        part_rows = pl.ds(k * kpart, kpart)
        return pltpu.make_async_copy(enc_hbm.at[part_rows], enc_v.at[part_rows], enc_sem.at[k])

    loads = [
        pltpu.make_async_copy(src_hbm, src_v, load_sem.at[0]),
        pltpu.make_async_copy(dec_hbm, dec_v, load_sem.at[1]),
        pltpu.make_async_copy(tgt_hbm.at[rows_of(z), my_cols], tgt_v, load_sem.at[2]),
        pltpu.make_async_copy(src_hbm.at[own_half, dcols(t)], srcd.at[t, own_half], load_sem.at[3]),
        pltpu.make_async_copy(bias_hbm, bias_ref, load_sem.at[4]),
        pltpu.make_async_copy(act_hbm, act_ref, load_sem.at[5]),
    ]
    loads[0].start()
    for k in range(enc_parts):
        load_enc(k).start()
    for load in loads[1:]:
        load.start()

    barrier = pltpu.get_barrier_semaphore()
    for k in range(1, nt):
        pl.semaphore_signal(barrier, inc=1, device_id=(lax.rem(t + k, nt), f), device_id_type=MESH)
    for peer in (z_up, z_down, sibling, y_peer):
        pl.semaphore_signal(barrier, inc=1, device_id=peer, device_id_type=MESH)
    pl.semaphore_wait(barrier, nt - 1 + 4)

    for load in (loads[0], loads[4], loads[5]):
        load.wait()
    acc[...] = jnp.broadcast_to(bias_ref[...][None, :], acc.shape)
    for k in range(enc_parts):
        load_enc(k).wait()
        part_rows = pl.ds(k * kpart, kpart)
        acc[...] += jnp.dot(src_v[:, part_rows], enc_v[part_rows, :], preferred_element_type=F32)

    for tile in range(rows // TILE):
        listed = act_ref[tile : tile + 1, :]
        for blk in range(cols // BLOCK):
            block_id = f * (cols // BLOCK) + blk
            active = jnp.max(jnp.where(listed == block_id, 1.0, 0.0), axis=1, keepdims=True)
            at = (pl.ds(tile * TILE, TILE), pl.ds(blk * BLOCK, BLOCK))
            v = acc[at]
            cdf = 0.5 * (1.0 + lax.erf(v * math.sqrt(0.5)))
            pdf = jnp.exp(-0.5 * v * v) * (1.0 / math.sqrt(2.0 * math.pi))
            fa[t, at[0], at[1]] = (v * cdf * active).astype(BF16)
            slope[at] = (cdf + v * pdf) * active

    def gather_start(part, send, y_sem, p_sem, m_sem):
        for k in range(1, ny):
            remote(part(t), part(t), send, y_sem.at[k], (tid(x, yl + k), f))
        gather_x(part, send, p_sem, m_sem, 0)

    def gather_x(part, send, p_sem, m_sem, k):
        own = part(tid(x, yl - k))
        remote(own, own, send, p_sem.at[k], (tid(x + 1, yl), f))
        remote(own, own, send, m_sem.at[k], (tid(x - 1, yl), f))

    def gather_y(part, send, y_sem, p_sem, m_sem):
        for k in range(1, ny):
            await_bytes(part(tid(x, yl - k)), y_sem.at[k])
            gather_x(part, send, p_sem, m_sem, k)

    def gather_relay(part, send, p_sem, m_sem, r_sem):
        for k in range(ny):
            below, above = part(tid(x - 1, yl - k)), part(tid(x + 1, yl - k))
            if k < ny // 2:
                await_bytes(below, p_sem.at[k])
                remote(below, below, send, r_sem.at[k], (tid(x + 1, yl), f))
                await_bytes(above, m_sem.at[k])
            else:
                await_bytes(above, m_sem.at[k])
                remote(above, above, send, r_sem.at[k], (tid(x - 1, yl), f))
                await_bytes(below, p_sem.at[k])

    def gather_far(part, r_sem):
        for k in range(ny):
            await_bytes(part(tid(x + 2, yl - k)), r_sem.at[k])

    hops_of = (n_minus // 3, 2 * n_minus // 3, n_minus)
    ends = [min(2 * hops + 1, nz) for hops in hops_of]
    starts = [0] + ends[:2]
    cuts = [pl.ds(a * chunk, (b - a) * chunk) for a, b in zip(starts, ends)]
    last = len(cuts) - 1

    def place_of(hop):
        return 2 * hop if hop >= 0 else -2 * hop - 1

    def hop_at(place):
        return -(place + 1) // 2 if place % 2 else place // 2


    def features_of(g):
        return fa.at[g]

    def grads_of(h):
        return lambda g: ga.at[g, cuts[h]]

    gather_start(features_of, f_send.at[0], f_y, f_p, f_m)

    for k in range(1, nt):
        to = lax.rem(t + k, nt)
        remote(src_hbm.at[own_half, dcols(to)], srcd.at[t, own_half], xs_sem.at[0], xs_sem.at[1], (to, f))

    loads[1].wait()

    @pl.loop(0, n_tiles)
    def _(n):
        at = pl.ds(pl.multiple_of(n * tile_w, tile_w), tile_w)
        full = pl.ds(pl.multiple_of(half * (1 - c) + n * tile_w, tile_w), tile_w)
        psend[:, at] = jnp.dot(fa[t], dec_v[:, full], preferred_element_type=F32).astype(BF16)
        remote(psend.at[:, at], precv.at[:, at], ps_send.at[0], ps_recv.at[n], sibling)

    @pl.loop(0, n_tiles)
    def _(n):
        at = pl.ds(pl.multiple_of(n * tile_w, tile_w), tile_w)
        full = pl.ds(pl.multiple_of(half * c + n * tile_w, tile_w), tile_w)
        part[:, at] = jnp.dot(fa[t], dec_v[:, full], preferred_element_type=F32)

    @pl.loop(0, n_tiles)
    def _(n):
        at = pl.ds(pl.multiple_of(n * tile_w, tile_w), tile_w)
        await_bytes(precv.at[:, at], ps_recv.at[n])
        part[:, at] += precv[:, at].astype(F32)

    def rs_step(slot, prev, owner, sub, device):
        value = part[rows_of(owner), pl.ds(sub * sub_w, sub_w)]
        if prev is not None:
            await_bytes(rrecv.at[prev, sub], rs_recv.at[prev, sub])
            value = value + rrecv[prev, sub].astype(F32)
        rsend[slot, sub] = value.astype(BF16)
        remote(rsend.at[slot, sub], rrecv.at[slot, sub], rs_send.at[0], rs_recv.at[slot, sub], device)

    for s in range(n_minus):
        for sub in range(ns):
            rs_step(s, s - 1 if s else None, zmod(z - (n_minus - s)), sub, z_down)
            if s < n_plus:
                rs_step(n_minus + s, n_minus + s - 1 if s else None, zmod(z + (n_plus - s)), sub, z_up)
    for sub in range(ns):
        value = part[rows_of(z), pl.ds(sub * sub_w, sub_w)]
        for slot in (n_minus - 1, n_minus + n_plus - 1):
            await_bytes(rrecv.at[slot, sub], rs_recv.at[slot, sub])
            value = value + rrecv[slot, sub].astype(F32)
        ysend[sub] = value.astype(BF16)
        remote(ysend.at[sub], yrecv.at[sub], yh_send.at[0], yh_recv.at[sub], y_peer)

    own_rows = pl.ds(0, chunk)
    gather_y(features_of, f_send.at[0], f_y, f_p, f_m)
    for sub in range(ns):
        await_bytes(yrecv.at[sub], yh_recv.at[sub])
        recon = ysend[sub].astype(F32) + yrecv[sub].astype(F32)
        target = tgt_v[:, pl.ds(sub * sub_w, sub_w)] if sub else None
        if sub == 0:
            loads[2].wait()
            target = tgt_v[:, pl.ds(0, sub_w)]
        at = pl.ds(pl.multiple_of(half * c + sub * sub_w, sub_w), sub_w)
        err[own_rows, at] = (recon - target.astype(F32)).astype(BF16)

    def ring_start(piece_of, next_of, subs, send, p_sem, m_sem, sib_send, sib_recv):
        for sub in range(subs):
            piece = piece_of(0, sub)
            remote(piece, piece, sib_send, sib_recv, sibling)
            remote(piece, next_of(0, -1, sub), send, p_sem.at[0, sub], z_up)
            remote(piece, next_of(0, 1, sub), send, m_sem.at[0, sub], z_down)

    def ring_step(piece_of, next_of, subs, s, send, p_sem, m_sem, sib_send, sib_recv):
        arrived = []
        for sub in range(subs):
            for sem, sign, hops, device in ((p_sem, -1, n_minus, z_up), (m_sem, 1, n_plus, z_down)):
                if s <= hops:
                    piece = piece_of(sign * s, sub)
                    await_bytes(piece, sem.at[s - 1, sub])
                    if s < hops:
                        remote(piece, next_of(sign * s, sign, sub), send, sem.at[s, sub], device)
                    arrived.append(piece)
        for piece in arrived:
            remote(piece, piece, sib_send, sib_recv, sibling)

    err_w = half // e_subs

    def err_piece(hop, sub):
        at = pl.ds(place_of(hop) * chunk, chunk)
        return err.at[at, pl.ds(pl.multiple_of(half * c + err_w * sub, err_w), err_w)]

    def err_next(hop, sign, sub):
        return err_piece(hop + sign, sub)

    def errd_piece(hop, sub):
        return errd.at[my_groups, zmod(z + hop)]

    def errd_next(hop, sign, sub):
        return errd_piece(hop, sub)

    e_ring = (e_zs.at[0], e_zp, e_zm, e_sib.at[0])
    d_ring = (d_zs.at[0], d_zp, d_zm, d_sib.at[0], d_sib.at[1])
    mine = t // (nt // 2) == c

    def errd_send():
        await_bytes(err.at[own_rows, my_cols], e_sib.at[1])

        @pl.when(mine)
        def _():
            for k in range(1, nt):
                to = lax.rem(t + k, nt)
                remote(err.at[own_rows, dcols(to)], errd.at[t, z], d_xs.at[0], d_xs.at[1], (to, f))
            errd[t, z] = err[own_rows, dcols(t)]

    def errd_start():
        @pl.when(mine)
        def _():
            await_bytes(errd.at[pl.ds(0, nt // 2 - 1), 0], d_xs.at[1])

        @pl.when(jnp.logical_not(mine))
        def _():
            await_bytes(errd.at[pl.ds(0, nt // 2), 0], d_xs.at[1])

        ring_start(errd_piece, errd_next, 1, *d_ring)

    def errd_step(s):
        ring_step(errd_piece, errd_next, 1, s, *d_ring[:4], d_sib.at[1 if s <= d_first else 2])

    def rows_at(place):
        return rows_of(zmod(z + hop_at(place)))

    def g_sems(h):
        return g_send.at[h], g_y.at[h], g_p.at[h], g_m.at[h]

    def g_relay(h):
        gather_relay(grads_of(h), g_send.at[h], g_p.at[h], g_m.at[h], g_r.at[h])

    def back(h):
        acc[cuts[h], :] = jnp.zeros((cuts[h].size, cols), F32)

        @pl.loop(0, enc_parts)
        def _(k):
            at = pl.ds(pl.multiple_of(k * kpart, kpart), kpart)
            acc[cuts[h], :] += lax.dot_general(
                err[cuts[h], at], dec_v[:, at], (((1,), (1,)), ((), ())), preferred_element_type=F32
            )

        for place in range(starts[h], ends[h]):
            at = pl.ds(place * chunk, chunk)
            ga[t, at, :] = (acc[at, :] * slope[rows_at(place), :]).astype(BF16)
        if h < last:
            gather_start(grads_of(h), *g_sems(h))
        else:
            for k in range(1, nt):
                remote(ga.at[t, cuts[h]], ga.at[t, cuts[h]], g_all.at[0], g_all.at[1], (lax.rem(t + k, nt), f))

    ring_start(err_piece, err_next, e_subs, *e_ring, e_sib.at[1])
    across = (((0,), (0,)), ((), ()))
    genc_ref[...] = jnp.zeros_like(genc_ref)
    gdec_ref[...] = jnp.zeros_like(gdec_ref)

    def dec_terms(hop):
        zz = zmod(z + hop)
        feats = jnp.concatenate([fa[g, rows_of(zz), :] for g in range(nt)], axis=0)
        errs = jnp.concatenate([errd[g, zz] for g in range(nt)], axis=0)
        gdec_ref[...] += lax.dot_general(feats, errs, across, preferred_element_type=F32)

    def dec_hops(first, stop):
        for hop in range(first, stop):
            for signed in ((0,) if hop == 0 else (-hop, hop) if hop <= n_plus else (-hop,)):
                dec_terms(signed)

    def enc_groups(dx):
        @pl.loop(0, ny)
        def _(k):
            g = tid(x + dx, yl - k)
            source = jnp.concatenate([srcd[g, rows_at(place), :] for place in range(starts[last])], axis=0)
            grads = ga[g, pl.ds(0, starts[last] * chunk), :]
            genc_ref[...] += lax.dot_general(source, grads, across, preferred_element_type=F32)

    def enc_late():
        @pl.loop(0, nt // 4)
        def _(n):
            groups = [n * 4 + k for k in range(4)]
            source = jnp.concatenate(
                [srcd[g, rows_at(place), :] for g in groups for place in range(starts[last], nz)], axis=0
            )
            grads = jnp.concatenate([ga[g, cuts[last], :] for g in groups], axis=0)
            genc_ref[...] += lax.dot_general(source, grads, across, preferred_element_type=F32)

    def loss_rows(h):
        for place in range(starts[h], ends[h]):
            total = jnp.zeros((16, 128), F32)
            for r in range(chunk // 16):
                for k in range(width // 128):
                    piece = err[pl.ds(place * chunk + r * 16, 16), pl.ds(k * 128, 128)].astype(F32)
                    total = total + piece * piece
            lpart[zmod(z + hop_at(place))] = total[:8] + total[8:]

    def loss_send():
        total = lpart[0]
        for k in range(1, nz):
            total = total + lpart[k]
        lbuf[t] = total
        for k in range(1, nt):
            remote(lbuf.at[t], lbuf.at[t], l_sem.at[0], l_sem.at[1], (lax.rem(t + k, nt), f))

    def sibling_errors(h):
        first = max(starts[h], 1)
        await_bytes(err.at[pl.ds(0, (ends[h] - first) * chunk), pl.ds(0, half)], e_sib.at[2 + h])

    d_lag = 3
    d_first = n_minus - d_lag
    for s in range(1, n_minus + 1):
        h = [s <= hops for hops in hops_of].index(True)
        ring_step(err_piece, err_next, e_subs, s, *e_ring, e_sib.at[2 + h])
        if s > d_lag:
            errd_step(s - d_lag)
        if s == 1:
            errd_send()
        if s == n_minus:
            gather_y(grads_of(1), *g_sems(1))
            g_relay(0)
        if s == hops_of[h]:
            sibling_errors(h)
            back(h)
        if s == d_lag - 1:
            errd_start()
        if s in (3, 5):
            loss_rows(h - 1)
        if s == 3:
            gather_relay(features_of, f_send.at[0], f_p, f_m, f_r)
        if s == 5:
            gather_y(grads_of(0), *g_sems(0))
            loads[3].wait()
            await_bytes(srcd.at[pl.ds(0, nt - 1), pl.ds(0, hrow)], xs_sem.at[1])
            remote(srcd.at[:, own_half], srcd.at[:, own_half], sf_sem.at[0], sf_sem.at[1], sibling)

    errd_step(d_first + 1)
    loss_rows(last)
    loss_send()
    gather_far(features_of, f_r)
    await_bytes(errd.at[pl.ds(0, nt // 2), pl.ds(0, 2 * d_first + 1)], d_sib.at[1])
    dec_hops(0, d_first + 1)
    errd_step(d_first + 2)
    await_bytes(srcd.at[:, sib_half], sf_sem.at[1])
    enc_groups(0)
    g_relay(1)
    errd_step(d_first + 3)
    enc_groups(1)
    enc_groups(-1)
    await_bytes(lbuf.at[pl.ds(0, nt - 1)], l_sem.at[1])
    sums = lbuf[0]
    for k in range(1, nt):
        sums = sums + lbuf[k]
    loss_ref[0, 0] = jnp.sum(sums) / (rows * nt * width)
    await_bytes(errd.at[pl.ds(0, nt // 2), pl.ds(0, nz - 2 * d_first - 1)], d_sib.at[2])
    dec_hops(d_first + 1, n_minus + 1)
    for h in range(last):
        gather_far(grads_of(h), g_r.at[h])
    enc_groups(2)
    await_bytes(ga.at[pl.ds(0, nt - 1), cuts[last]], g_all.at[1])
    enc_late()

    await_bytes(srcd.at[pl.ds(0, nt - 1), pl.ds(0, hrow)], xs_sem.at[0])
    await_bytes(srcd.at[:, own_half], sf_sem.at[0])
    await_bytes(fa.at[pl.ds(0, nt - 1)], f_send.at[0])
    for h in range(last):
        await_bytes(ga.at[pl.ds(0, nt - 1), cuts[h]], g_send.at[h])
    await_bytes(ga.at[pl.ds(0, nt - 1), cuts[last]], g_all.at[0])
    await_bytes(psend, ps_send.at[0])
    await_bytes(rsend, rs_send.at[0])
    await_bytes(ysend, yh_send.at[0])
    await_bytes(err.at[pl.ds(0, rows - chunk), pl.ds(0, half)], e_zs.at[0])
    await_bytes(err.at[:, pl.ds(0, half)], e_sib.at[0])
    await_bytes(errd.at[pl.ds(0, nt // 2), pl.ds(0, nz - 1)], d_zs.at[0])
    await_bytes(errd.at[pl.ds(0, nt // 2)], d_sib.at[0])
    await_bytes(lbuf.at[pl.ds(0, nt - 1)], l_sem.at[0])

    @pl.when(mine)
    def _():
        await_bytes(errd.at[pl.ds(0, nt - 1), 0], d_xs.at[0])


def on_device(nt, nf, ns, e_subs, source_acts, target_acts, enc_weight, enc_bias, dec_weight, active_blocks):
    rows, width = source_acts.shape
    cols = enc_weight.shape[1]
    ny, nz = nt // NX, nf // PER_Z
    half, dblk, chunk = width // 2, width // nt, rows // nz
    enc_parts, n_tiles = 4, 4
    n_minus, n_plus = nz // 2, (nz - 1) // 2
    dma = lambda *shape: pltpu.SemaphoreType.DMA(shape)
    scratch = [
        pltpu.VMEM((rows, width), BF16),
        pltpu.VMEM((width, cols), BF16),
        pltpu.VMEM((cols, width), BF16),
        pltpu.VMEM((cols,), F32),
        pltpu.VMEM(active_blocks.shape, jnp.int32),
        pltpu.VMEM((chunk, half), BF16),
        pltpu.VMEM((rows, cols), F32),
        pltpu.VMEM((rows, cols), F32),
        pltpu.VMEM((nt, rows, dblk), BF16),
        pltpu.VMEM((nt, rows, cols), BF16),
        pltpu.VMEM((nt, rows, cols), BF16),
        pltpu.VMEM((rows, width), BF16),
        pltpu.VMEM((nt, nz, chunk, dblk), BF16),
        pltpu.VMEM((rows, half), F32),
        pltpu.VMEM((rows, half), BF16),
        pltpu.VMEM((rows, half), BF16),
        pltpu.VMEM((nz - 1, ns, chunk, half // ns), BF16),
        pltpu.VMEM((nz - 1, ns, chunk, half // ns), BF16),
        pltpu.VMEM((ns, chunk, half // ns), BF16),
        pltpu.VMEM((ns, chunk, half // ns), BF16),
        pltpu.VMEM((nt, 8, 128), F32),
        pltpu.VMEM((nz, 8, 128), F32),
        dma(6), dma(enc_parts), dma(2), dma(2),
        dma(1), dma(ny), dma(ny), dma(ny), dma(ny),
        dma(2), dma(2, ny), dma(2, ny), dma(2, ny), dma(2, ny), dma(2),
        dma(1), dma(n_tiles),
        dma(1), dma(nz - 1, ns), dma(1), dma(ns),
        dma(1), dma(n_minus, e_subs), dma(n_plus, e_subs), dma(5),
        dma(2), dma(1), dma(n_minus, 1), dma(n_plus, 1), dma(3),
        dma(2),
    ]
    vmem = pl.BlockSpec(memory_space=pltpu.VMEM)
    hbm = pl.BlockSpec(memory_space=pltpu.HBM)
    grad_encoder, grad_decoder, loss = pl.pallas_call(
        functools.partial(kernel, (nt, ny, nz, rows, width, cols, ns, e_subs)),
        out_shape=(
            jax.ShapeDtypeStruct((dblk, cols), F32),
            jax.ShapeDtypeStruct((cols, dblk), F32),
            jax.ShapeDtypeStruct((1, 1), F32),
        ),
        in_specs=[hbm] * 6,
        out_specs=(vmem, vmem, pl.BlockSpec(memory_space=pltpu.SMEM)),
        scratch_shapes=scratch,
        compiler_params=pltpu.CompilerParams(
            collective_id=0, has_side_effects=True, vmem_limit_bytes=60 * 1024 * 1024
        ),
        name="step",
    )(source_acts, target_acts, enc_weight, enc_bias, dec_weight, active_blocks)
    return grad_encoder, grad_decoder, loss.reshape(())


def solution(mesh):
    placed = (
        P("tok", None),
        P("tok", None),
        P(None, "feat"),
        P("feat"),
        P("feat", None),
        P("tok", None),
    )
    return jax.shard_map(
        functools.partial(on_device, mesh.shape["tok"], mesh.shape["feat"], 2, 2),
        mesh=mesh,
        in_specs=placed,
        out_specs=(P("tok", "feat"), P("feat", "tok"), P()),
        check_vma=False,
    )
```

```python
import functools
import math

import jax
import jax.numpy as jnp
from jax import lax
from jax.experimental import pallas as pl
from jax.experimental.pallas import tpu as pltpu
from jax.sharding import PartitionSpec as P

BLOCK = 128
TILE = 64
NX = 4
PER_Z = 4
MESH = pl.DeviceIdType.MESH
F32 = jnp.float32
BF16 = jnp.bfloat16


def remote(src, dst, send_sem, recv_sem, device):
    pltpu.make_async_remote_copy(
        src_ref=src, dst_ref=dst, send_sem=send_sem, recv_sem=recv_sem, device_id=device, device_id_type=MESH
    ).start()


def await_bytes(ref, sem):
    pltpu.make_async_copy(ref, ref, sem).wait()


def kernel(dims, src_hbm, tgt_hbm, enc_hbm, bias_hbm, dec_hbm, act_hbm, genc_ref, gdec_ref, loss_ref, *scratch):
    nt, ny, nz, rows, width, cols, ns, e_subs = dims
    (src_v, enc_v, dec_v, bias_ref, act_ref, tgt_v, acc, slope, srcd, fa, ga, err, errd, part, psend, precv, rsend, rrecv, ysend, yrecv, lbuf, lpart,
     load_sem, enc_sem, xs_sem, sf_sem, f_send, f_y, f_p, f_m, f_r, g_send, g_y, g_p, g_m, g_r, g_all, ps_send, ps_recv,
     rs_send, rs_recv, yh_send, yh_recv, e_zs, e_zp, e_zm, e_sib, d_xs, d_zs, d_zp, d_zm, d_sib, l_sem) = scratch
    half = width // 2
    dblk = width // nt
    chunk = rows // nz
    hrow = rows // 2
    sub_w = half // ns
    n_minus, n_plus = nz // 2, (nz - 1) // 2
    enc_parts = enc_sem.shape[0]
    kpart = width // enc_parts
    n_tiles = ps_recv.shape[0]
    tile_w = half // n_tiles

    t, f = lax.axis_index("tok"), lax.axis_index("feat")
    x, yl = t // ny, t % ny
    z, yh, c = f // PER_Z, (f // 2) % 2, f % 2

    def zmod(v):
        return lax.rem(v + nz, nz)

    def fid(zz, hh, cc):
        return (zz * 2 + hh) * 2 + cc

    def tid(xx, yy):
        return lax.rem(xx + NX, NX) * ny + lax.rem(yy + ny, ny)

    def rows_of(zz):
        return pl.ds(pl.multiple_of(zz * chunk, chunk), chunk)

    def dcols(tt):
        return pl.ds(pl.multiple_of(tt * dblk, dblk), dblk)

    z_up, z_down = (t, fid(zmod(z + 1), yh, c)), (t, fid(zmod(z - 1), yh, c))
    sibling, y_peer = (t, fid(z, yh, 1 - c)), (t, fid(z, 1 - yh, c))
    own_half = pl.ds(pl.multiple_of(hrow * c, hrow), hrow)
    sib_half = pl.ds(pl.multiple_of(hrow * (1 - c), hrow), hrow)
    my_cols = pl.ds(pl.multiple_of(half * c, half), half)
    my_groups = pl.ds(c * (nt // 2), nt // 2)

    def load_enc(k):
        part_rows = pl.ds(k * kpart, kpart)
        return pltpu.make_async_copy(enc_hbm.at[part_rows], enc_v.at[part_rows], enc_sem.at[k])

    loads = [
        pltpu.make_async_copy(src_hbm, src_v, load_sem.at[0]),
        pltpu.make_async_copy(dec_hbm, dec_v, load_sem.at[1]),
        pltpu.make_async_copy(tgt_hbm.at[rows_of(z), my_cols], tgt_v, load_sem.at[2]),
        pltpu.make_async_copy(src_hbm.at[own_half, dcols(t)], srcd.at[t, own_half], load_sem.at[3]),
        pltpu.make_async_copy(bias_hbm, bias_ref, load_sem.at[4]),
        pltpu.make_async_copy(act_hbm, act_ref, load_sem.at[5]),
    ]
    loads[0].start()
    for k in range(enc_parts):
        load_enc(k).start()
    for load in loads[1:]:
        load.start()

    barrier = pltpu.get_barrier_semaphore()
    for k in range(1, nt):
        pl.semaphore_signal(barrier, inc=1, device_id=(lax.rem(t + k, nt), f), device_id_type=MESH)
    for peer in (z_up, z_down, sibling, y_peer):
        pl.semaphore_signal(barrier, inc=1, device_id=peer, device_id_type=MESH)

    for load in (loads[0], loads[4], loads[5]):
        load.wait()
    acc[...] = jnp.broadcast_to(bias_ref[...][None, :], acc.shape)
    for k in range(enc_parts):
        load_enc(k).wait()
        part_rows = pl.ds(k * kpart, kpart)
        acc[...] += jnp.dot(src_v[:, part_rows], enc_v[part_rows, :], preferred_element_type=F32)

    for tile in range(rows // TILE):
        listed = act_ref[tile : tile + 1, :]
        for blk in range(cols // BLOCK):
            block_id = f * (cols // BLOCK) + blk
            active = jnp.max(jnp.where(listed == block_id, 1.0, 0.0), axis=1, keepdims=True)
            at = (pl.ds(tile * TILE, TILE), pl.ds(blk * BLOCK, BLOCK))
            v = acc[at]
            cdf = 0.5 * (1.0 + lax.erf(v * math.sqrt(0.5)))
            pdf = jnp.exp(-0.5 * v * v) * (1.0 / math.sqrt(2.0 * math.pi))
            fa[t, at[0], at[1]] = (v * cdf * active).astype(BF16)
            slope[at] = (cdf + v * pdf) * active

    def gather_start(part, send, y_sem, p_sem, m_sem):
        for k in range(1, ny):
            remote(part(t), part(t), send, y_sem.at[k], (tid(x, yl + k), f))
        gather_x(part, send, p_sem, m_sem, 0)

    def gather_x(part, send, p_sem, m_sem, k):
        own = part(tid(x, yl - k))
        remote(own, own, send, p_sem.at[k], (tid(x + 1, yl), f))
        remote(own, own, send, m_sem.at[k], (tid(x - 1, yl), f))

    def gather_y(part, send, y_sem, p_sem, m_sem):
        for k in range(1, ny):
            await_bytes(part(tid(x, yl - k)), y_sem.at[k])
            gather_x(part, send, p_sem, m_sem, k)

    def gather_relay(part, send, p_sem, m_sem, r_sem):
        for k in range(ny):
            below, above = part(tid(x - 1, yl - k)), part(tid(x + 1, yl - k))
            if k < ny // 2:
                await_bytes(below, p_sem.at[k])
                remote(below, below, send, r_sem.at[k], (tid(x + 1, yl), f))
                await_bytes(above, m_sem.at[k])
            else:
                await_bytes(above, m_sem.at[k])
                remote(above, above, send, r_sem.at[k], (tid(x - 1, yl), f))
                await_bytes(below, p_sem.at[k])

    def gather_far(part, r_sem):
        for k in range(ny):
            await_bytes(part(tid(x + 2, yl - k)), r_sem.at[k])

    hops_of = (n_minus // 3, 2 * n_minus // 3, n_minus)
    ends = [min(2 * hops + 1, nz) for hops in hops_of]
    starts = [0] + ends[:2]
    cuts = [pl.ds(a * chunk, (b - a) * chunk) for a, b in zip(starts, ends)]
    last = len(cuts) - 1

    def place_of(hop):
        return 2 * hop if hop >= 0 else -2 * hop - 1

    def hop_at(place):
        return -(place + 1) // 2 if place % 2 else place // 2


    def features_of(g):
        return fa.at[g]

    def grads_of(h):
        return lambda g: ga.at[g, cuts[h]]

    pl.semaphore_wait(barrier, nt - 1 + 4)
    gather_start(features_of, f_send.at[0], f_y, f_p, f_m)

    loads[1].wait()

    @pl.loop(0, n_tiles)
    def _(n):
        at = pl.ds(pl.multiple_of(n * tile_w, tile_w), tile_w)
        full = pl.ds(pl.multiple_of(half * (1 - c) + n * tile_w, tile_w), tile_w)
        psend[:, at] = jnp.dot(fa[t], dec_v[:, full], preferred_element_type=F32).astype(BF16)
        remote(psend.at[:, at], precv.at[:, at], ps_send.at[0], ps_recv.at[n], sibling)

    @pl.loop(0, n_tiles)
    def _(n):
        at = pl.ds(pl.multiple_of(n * tile_w, tile_w), tile_w)
        full = pl.ds(pl.multiple_of(half * c + n * tile_w, tile_w), tile_w)
        part[:, at] = jnp.dot(fa[t], dec_v[:, full], preferred_element_type=F32)

    @pl.loop(0, n_tiles)
    def _(n):
        at = pl.ds(pl.multiple_of(n * tile_w, tile_w), tile_w)
        await_bytes(precv.at[:, at], ps_recv.at[n])
        part[:, at] += precv[:, at].astype(F32)

    def rs_step(slot, prev, owner, sub, device):
        value = part[rows_of(owner), pl.ds(sub * sub_w, sub_w)]
        if prev is not None:
            await_bytes(rrecv.at[prev, sub], rs_recv.at[prev, sub])
            value = value + rrecv[prev, sub].astype(F32)
        rsend[slot, sub] = value.astype(BF16)
        remote(rsend.at[slot, sub], rrecv.at[slot, sub], rs_send.at[0], rs_recv.at[slot, sub], device)

    for s in range(n_minus):
        for sub in range(ns):
            rs_step(s, s - 1 if s else None, zmod(z - (n_minus - s)), sub, z_down)
            if s < n_plus:
                rs_step(n_minus + s, n_minus + s - 1 if s else None, zmod(z + (n_plus - s)), sub, z_up)
        if s == 0:
            for k in range(1, nt):
                to = lax.rem(t + k, nt)
                remote(src_hbm.at[own_half, dcols(to)], srcd.at[t, own_half], xs_sem.at[0], xs_sem.at[1], (to, f))
    for sub in range(ns):
        value = part[rows_of(z), pl.ds(sub * sub_w, sub_w)]
        for slot in (n_minus - 1, n_minus + n_plus - 1):
            await_bytes(rrecv.at[slot, sub], rs_recv.at[slot, sub])
            value = value + rrecv[slot, sub].astype(F32)
        ysend[sub] = value.astype(BF16)
        remote(ysend.at[sub], yrecv.at[sub], yh_send.at[0], yh_recv.at[sub], y_peer)

    own_rows = pl.ds(0, chunk)
    gather_y(features_of, f_send.at[0], f_y, f_p, f_m)
    for sub in range(ns):
        await_bytes(yrecv.at[sub], yh_recv.at[sub])
        recon = ysend[sub].astype(F32) + yrecv[sub].astype(F32)
        target = tgt_v[:, pl.ds(sub * sub_w, sub_w)] if sub else None
        if sub == 0:
            loads[2].wait()
            target = tgt_v[:, pl.ds(0, sub_w)]
        at = pl.ds(pl.multiple_of(half * c + sub * sub_w, sub_w), sub_w)
        err[own_rows, at] = (recon - target.astype(F32)).astype(BF16)

    def ring_start(piece_of, next_of, subs, send, p_sem, m_sem, sib_send, sib_recv):
        for sub in range(subs):
            piece = piece_of(0, sub)
            remote(piece, piece, sib_send, sib_recv, sibling)
            remote(piece, next_of(0, -1, sub), send, p_sem.at[0, sub], z_up)
            remote(piece, next_of(0, 1, sub), send, m_sem.at[0, sub], z_down)

    def ring_step(piece_of, next_of, subs, s, send, p_sem, m_sem, sib_send, sib_recv):
        arrived = []
        for sub in range(subs):
            for sem, sign, hops, device in ((p_sem, -1, n_minus, z_up), (m_sem, 1, n_plus, z_down)):
                if s <= hops:
                    piece = piece_of(sign * s, sub)
                    await_bytes(piece, sem.at[s - 1, sub])
                    if s < hops:
                        remote(piece, next_of(sign * s, sign, sub), send, sem.at[s, sub], device)
                    arrived.append(piece)
        for piece in arrived:
            remote(piece, piece, sib_send, sib_recv, sibling)

    err_w = half // e_subs

    def err_piece(hop, sub):
        at = pl.ds(place_of(hop) * chunk, chunk)
        return err.at[at, pl.ds(pl.multiple_of(half * c + err_w * sub, err_w), err_w)]

    def err_next(hop, sign, sub):
        return err_piece(hop + sign, sub)

    def errd_piece(hop, sub):
        return errd.at[my_groups, zmod(z + hop)]

    def errd_next(hop, sign, sub):
        return errd_piece(hop, sub)

    e_ring = (e_zs.at[0], e_zp, e_zm, e_sib.at[0])
    d_ring = (d_zs.at[0], d_zp, d_zm, d_sib.at[0], d_sib.at[1])
    mine = t // (nt // 2) == c

    def errd_send():
        await_bytes(err.at[own_rows, my_cols], e_sib.at[1])

        @pl.when(mine)
        def _():
            for k in range(1, nt):
                to = lax.rem(t + k, nt)
                remote(err.at[own_rows, dcols(to)], errd.at[t, z], d_xs.at[0], d_xs.at[1], (to, f))
            errd[t, z] = err[own_rows, dcols(t)]

    def errd_start():
        @pl.when(mine)
        def _():
            await_bytes(errd.at[pl.ds(0, nt // 2 - 1), 0], d_xs.at[1])

        @pl.when(jnp.logical_not(mine))
        def _():
            await_bytes(errd.at[pl.ds(0, nt // 2), 0], d_xs.at[1])

        ring_start(errd_piece, errd_next, 1, *d_ring)

    def errd_step(s):
        ring_step(errd_piece, errd_next, 1, s, *d_ring[:4], d_sib.at[1 if s <= d_first else 2])

    def rows_at(place):
        return rows_of(zmod(z + hop_at(place)))

    def g_sems(h):
        return g_send.at[h], g_y.at[h], g_p.at[h], g_m.at[h]

    def g_relay(h):
        gather_relay(grads_of(h), g_send.at[h], g_p.at[h], g_m.at[h], g_r.at[h])

    def back(h):
        acc[cuts[h], :] = jnp.zeros((cuts[h].size, cols), F32)

        @pl.loop(0, enc_parts)
        def _(k):
            at = pl.ds(pl.multiple_of(k * kpart, kpart), kpart)
            acc[cuts[h], :] += lax.dot_general(
                err[cuts[h], at], dec_v[:, at], (((1,), (1,)), ((), ())), preferred_element_type=F32
            )

        for place in range(starts[h], ends[h]):
            at = pl.ds(place * chunk, chunk)
            ga[t, at, :] = (acc[at, :] * slope[rows_at(place), :]).astype(BF16)
        if h < last:
            gather_start(grads_of(h), *g_sems(h))
        else:
            for k in range(1, nt):
                remote(ga.at[t, cuts[h]], ga.at[t, cuts[h]], g_all.at[0], g_all.at[1], (lax.rem(t + k, nt), f))

    ring_start(err_piece, err_next, e_subs, *e_ring, e_sib.at[1])
    across = (((0,), (0,)), ((), ()))
    genc_ref[...] = jnp.zeros_like(genc_ref)
    gdec_ref[...] = jnp.zeros_like(gdec_ref)

    def dec_terms(hop):
        zz = zmod(z + hop)
        feats = jnp.concatenate([fa[g, rows_of(zz), :] for g in range(nt)], axis=0)
        errs = jnp.concatenate([errd[g, zz] for g in range(nt)], axis=0)
        gdec_ref[...] += lax.dot_general(feats, errs, across, preferred_element_type=F32)

    def dec_hops(first, stop):
        for hop in range(first, stop):
            for signed in ((0,) if hop == 0 else (-hop, hop) if hop <= n_plus else (-hop,)):
                dec_terms(signed)

    def enc_groups(dx):
        @pl.loop(0, ny)
        def _(k):
            g = tid(x + dx, yl - k)
            source = jnp.concatenate([srcd[g, rows_at(place), :] for place in range(starts[last])], axis=0)
            grads = ga[g, pl.ds(0, starts[last] * chunk), :]
            genc_ref[...] += lax.dot_general(source, grads, across, preferred_element_type=F32)

    def enc_late():
        @pl.loop(0, nt // 4)
        def _(n):
            groups = [n * 4 + k for k in range(4)]
            source = jnp.concatenate(
                [srcd[g, rows_at(place), :] for g in groups for place in range(starts[last], nz)], axis=0
            )
            grads = jnp.concatenate([ga[g, cuts[last], :] for g in groups], axis=0)
            genc_ref[...] += lax.dot_general(source, grads, across, preferred_element_type=F32)

    def loss_rows(h):
        for place in range(starts[h], ends[h]):
            total = jnp.zeros((16, 128), F32)
            for r in range(chunk // 16):
                for k in range(width // 128):
                    piece = err[pl.ds(place * chunk + r * 16, 16), pl.ds(k * 128, 128)].astype(F32)
                    total = total + piece * piece
            lpart[zmod(z + hop_at(place))] = total[:8] + total[8:]

    def loss_send():
        total = lpart[0]
        for k in range(1, nz):
            total = total + lpart[k]
        lbuf[t] = total
        for k in range(1, nt):
            remote(lbuf.at[t], lbuf.at[t], l_sem.at[0], l_sem.at[1], (lax.rem(t + k, nt), f))

    def sibling_errors(h):
        first = max(starts[h], 1)
        await_bytes(err.at[pl.ds(0, (ends[h] - first) * chunk), pl.ds(0, half)], e_sib.at[2 + h])

    d_lag = 3
    d_first = n_minus - d_lag
    for s in range(1, n_minus + 1):
        h = [s <= hops for hops in hops_of].index(True)
        ring_step(err_piece, err_next, e_subs, s, *e_ring, e_sib.at[2 + h])
        if s > d_lag:
            errd_step(s - d_lag)
        if s == 1:
            errd_send()
        if s == n_minus:
            gather_y(grads_of(1), *g_sems(1))
            g_relay(0)
        if s == hops_of[h]:
            sibling_errors(h)
            back(h)
        if s == d_lag - 1:
            errd_start()
        if s in (3, 5):
            loss_rows(h - 1)
        if s == 3:
            gather_relay(features_of, f_send.at[0], f_p, f_m, f_r)
        if s == 5:
            gather_y(grads_of(0), *g_sems(0))
            loads[3].wait()
            await_bytes(srcd.at[pl.ds(0, nt - 1), pl.ds(0, hrow)], xs_sem.at[1])
            remote(srcd.at[:, own_half], srcd.at[:, own_half], sf_sem.at[0], sf_sem.at[1], sibling)

    errd_step(d_first + 1)
    loss_rows(last)
    loss_send()
    gather_far(features_of, f_r)
    await_bytes(errd.at[pl.ds(0, nt // 2), pl.ds(0, 2 * d_first + 1)], d_sib.at[1])
    dec_hops(0, d_first + 1)
    errd_step(d_first + 2)
    await_bytes(srcd.at[:, sib_half], sf_sem.at[1])
    enc_groups(0)
    g_relay(1)
    errd_step(d_first + 3)
    enc_groups(1)
    enc_groups(-1)
    await_bytes(lbuf.at[pl.ds(0, nt - 1)], l_sem.at[1])
    sums = lbuf[0]
    for k in range(1, nt):
        sums = sums + lbuf[k]
    loss_ref[0, 0] = jnp.sum(sums) / (rows * nt * width)
    await_bytes(errd.at[pl.ds(0, nt // 2), pl.ds(0, nz - 2 * d_first - 1)], d_sib.at[2])
    dec_hops(d_first + 1, n_minus + 1)
    for h in range(last):
        gather_far(grads_of(h), g_r.at[h])
    enc_groups(2)
    await_bytes(ga.at[pl.ds(0, nt - 1), cuts[last]], g_all.at[1])
    enc_late()

    await_bytes(srcd.at[pl.ds(0, nt - 1), pl.ds(0, hrow)], xs_sem.at[0])
    await_bytes(srcd.at[:, own_half], sf_sem.at[0])
    await_bytes(fa.at[pl.ds(0, nt - 1)], f_send.at[0])
    for h in range(last):
        await_bytes(ga.at[pl.ds(0, nt - 1), cuts[h]], g_send.at[h])
    await_bytes(ga.at[pl.ds(0, nt - 1), cuts[last]], g_all.at[0])
    await_bytes(psend, ps_send.at[0])
    await_bytes(rsend, rs_send.at[0])
    await_bytes(ysend, yh_send.at[0])
    await_bytes(err.at[pl.ds(0, rows - chunk), pl.ds(0, half)], e_zs.at[0])
    await_bytes(err.at[:, pl.ds(0, half)], e_sib.at[0])
    await_bytes(errd.at[pl.ds(0, nt // 2), pl.ds(0, nz - 1)], d_zs.at[0])
    await_bytes(errd.at[pl.ds(0, nt // 2)], d_sib.at[0])
    await_bytes(lbuf.at[pl.ds(0, nt - 1)], l_sem.at[0])

    @pl.when(mine)
    def _():
        await_bytes(errd.at[pl.ds(0, nt - 1), 0], d_xs.at[0])


def on_device(nt, nf, ns, e_subs, source_acts, target_acts, enc_weight, enc_bias, dec_weight, active_blocks):
    rows, width = source_acts.shape
    cols = enc_weight.shape[1]
    ny, nz = nt // NX, nf // PER_Z
    half, dblk, chunk = width // 2, width // nt, rows // nz
    enc_parts, n_tiles = 4, 4
    n_minus, n_plus = nz // 2, (nz - 1) // 2
    dma = lambda *shape: pltpu.SemaphoreType.DMA(shape)
    scratch = [
        pltpu.VMEM((rows, width), BF16),
        pltpu.VMEM((width, cols), BF16),
        pltpu.VMEM((cols, width), BF16),
        pltpu.VMEM((cols,), F32),
        pltpu.VMEM(active_blocks.shape, jnp.int32),
        pltpu.VMEM((chunk, half), BF16),
        pltpu.VMEM((rows, cols), F32),
        pltpu.VMEM((rows, cols), F32),
        pltpu.VMEM((nt, rows, dblk), BF16),
        pltpu.VMEM((nt, rows, cols), BF16),
        pltpu.VMEM((nt, rows, cols), BF16),
        pltpu.VMEM((rows, width), BF16),
        pltpu.VMEM((nt, nz, chunk, dblk), BF16),
        pltpu.VMEM((rows, half), F32),
        pltpu.VMEM((rows, half), BF16),
        pltpu.VMEM((rows, half), BF16),
        pltpu.VMEM((nz - 1, ns, chunk, half // ns), BF16),
        pltpu.VMEM((nz - 1, ns, chunk, half // ns), BF16),
        pltpu.VMEM((ns, chunk, half // ns), BF16),
        pltpu.VMEM((ns, chunk, half // ns), BF16),
        pltpu.VMEM((nt, 8, 128), F32),
        pltpu.VMEM((nz, 8, 128), F32),
        dma(6), dma(enc_parts), dma(2), dma(2),
        dma(1), dma(ny), dma(ny), dma(ny), dma(ny),
        dma(2), dma(2, ny), dma(2, ny), dma(2, ny), dma(2, ny), dma(2),
        dma(1), dma(n_tiles),
        dma(1), dma(nz - 1, ns), dma(1), dma(ns),
        dma(1), dma(n_minus, e_subs), dma(n_plus, e_subs), dma(5),
        dma(2), dma(1), dma(n_minus, 1), dma(n_plus, 1), dma(3),
        dma(2),
    ]
    vmem = pl.BlockSpec(memory_space=pltpu.VMEM)
    hbm = pl.BlockSpec(memory_space=pltpu.HBM)
    grad_encoder, grad_decoder, loss = pl.pallas_call(
        functools.partial(kernel, (nt, ny, nz, rows, width, cols, ns, e_subs)),
        out_shape=(
            jax.ShapeDtypeStruct((dblk, cols), F32),
            jax.ShapeDtypeStruct((cols, dblk), F32),
            jax.ShapeDtypeStruct((1, 1), F32),
        ),
        in_specs=[hbm] * 6,
        out_specs=(vmem, vmem, pl.BlockSpec(memory_space=pltpu.SMEM)),
        scratch_shapes=scratch,
        compiler_params=pltpu.CompilerParams(
            collective_id=0, has_side_effects=True, vmem_limit_bytes=60 * 1024 * 1024
        ),
        name="step",
    )(source_acts, target_acts, enc_weight, enc_bias, dec_weight, active_blocks)
    return grad_encoder, grad_decoder, loss.reshape(())


def solution(mesh):
    placed = (
        P("tok", None),
        P("tok", None),
        P(None, "feat"),
        P("feat"),
        P("feat", None),
        P("tok", None),
    )
    return jax.shard_map(
        functools.partial(on_device, mesh.shape["tok"], mesh.shape["feat"], 2, 2),
        mesh=mesh,
        in_specs=placed,
        out_specs=(P("tok", "feat"), P("feat", "tok"), P()),
        check_vma=False,
    )
```
